32 devices in a mesh: layer: 4 (over y, x), slab: 8 (over z, core).
Axes of the slice: x: 2, y: 2, z: 4, core: 2. Of those that a mesh axis runs over, the one named last changes fastest.
Arguments:
- activations: bfloat16 [4, 256, 8192], P(None, ('layer', 'slab')), may hold values from -6 to 6
- gram_prior: float32 [4, 8192, 8192], P('layer', None, 'slab'), as said below
- targets: float32 [4, 8192, 128], P('layer', 'slab'), may hold values from -6 to 6
- ridge: float32 [4], P('layer'), may hold values from 0.5 to 2
Outputs:
- gram_new: float32 [4, 8192, 8192], P('layer', None, 'slab')
- probe_weights: float32 [4, 8192, 128], P('layer', 'slab')
- residual: float32 [4, 8192, 128], P('layer', 'slab')
The draws below stay inside these ranges and needn't reach their ends.
Inputs may be any that keep to these rules, and one draw needn't show every extreme that they name: `gram_prior`: each layer's matrix is exactly symmetric.
All inputs are finite; a program needn't handle non-finite values.
Results may differ from the reference program's by a relative error of at most 0.0003.
Values may be sent and summed in bfloat16 or wider, within the bound.
A program may use at most 256 MiB of HBM per device.

```python
import math
import jax
import jax.numpy as jnp
from jax import lax

D = 8192
R = 128
ITERS = 2
LAYERS = 4
TOKENS = 256


def draw_gram_prior(key, part):
    key = jax.random.fold_in(key, 11)
    noise_key, diag_key = jax.random.split(key)
    noise = jax.random.normal(noise_key, (LAYERS, D, D), jnp.float32)
    sym = (noise + jnp.swapaxes(noise, 1, 2)) * 0.7071
    diag = jax.random.uniform(diag_key, (LAYERS, D, 1), jnp.float32, 1.0, 4.0)
    spread = 0.4
    rows = lax.broadcasted_iota(jnp.int32, (D, D), 0)
    cols = lax.broadcasted_iota(jnp.int32, (D, D), 1)
    body_part = jnp.where(rows == cols, diag, spread * D ** (-0.5) * sym)
    return (TOKENS * body_part).astype(jnp.float32)


def levels(key, extent, pieces, low, high):
    gain = 1.0
    for axis_at, shards_of in pieces:
        heights = jax.random.uniform(jax.random.fold_in(jax.random.fold_in(key, 6), axis_at), (shards_of,), jnp.float32, low / len(pieces), high / len(pieces))
        gain = gain * jnp.repeat(jnp.exp(heights), extent[axis_at] // shards_of).reshape((-1,) + (1,) * (len(extent) - 1 - axis_at))
    return gain


def normal_values(rng, shape, width, most, pieces=(), kind=jnp.bfloat16):
    level = levels(rng, shape, pieces, -0.22, 0.18) if pieces else 1.0
    array = jax.random.normal(rng, shape, jnp.float32) * width * level
    return jnp.minimum(jnp.maximum(array, -most), most).astype(kind)


def setup_inputs(seed: int = 0) -> dict:
    splits = jax.random.split(jax.random.key(seed), 5)
    return {
        "activations": normal_values(splits[0], (LAYERS, TOKENS, D), 1.0, 6.0, ((1, 32),)),
        "gram_prior": draw_gram_prior(jax.random.fold_in(splits[4], 71), 0),
        "targets": normal_values(splits[2], (LAYERS, D, R), 1.0, 6.0, ((0, 4), (1, 8)), jnp.float32),
        "ridge": jnp.clip(jnp.exp(math.log(2.0) - 1.3862944 * jax.random.uniform(splits[3], (LAYERS,), jnp.float32) ** levels(splits[3], (LAYERS,), ((0, 4),), -0.2, 0.2)), 0.5, 2.0),
    }


def solve_layer(items):
    tokens_layer, prior, rhs, lam = items
    gram = prior + jnp.dot(tokens_layer.T, tokens_layer, preferred_element_type=jnp.float32)

    def apply_op(vecs):
        return jnp.dot(gram, vecs, precision=lax.Precision.HIGHEST, preferred_element_type=jnp.float32) / TOKENS + lam * vecs

    weights = jnp.zeros_like(rhs)
    resid = rhs
    direction = rhs
    norm_now = jnp.sum(resid * resid, axis=0)
    for step in range(ITERS):
        image = apply_op(direction)
        alpha = norm_now / jnp.sum(direction * image, axis=0)
        weights = weights + alpha * direction
        resid = resid - alpha * image
        norm_next = jnp.sum(resid * resid, axis=0)
        direction = resid + (norm_next / norm_now) * direction
        norm_now = norm_next
    return gram, weights, resid


def reference(activations, gram_prior, targets, ridge):
    gram_new, probe_weights, residual = lax.map(solve_layer, (activations, gram_prior, targets, ridge))
    return gram_new, probe_weights, residual
```

```python
import functools
import jax
import jax.numpy as jnp
from jax import lax
from jax.experimental import pallas as pl
from jax.experimental.pallas import tpu as pltpu
from jax.sharding import PartitionSpec as P

MESH = pl.DeviceIdType.MESH
F32 = jnp.float32
BF16 = jnp.bfloat16


def split(x):
    hi = x.astype(BF16)
    return hi, (x - hi.astype(F32)).astype(BF16)


def dot(a, b, dims=((1,), (0,))):
    return lax.dot_general(a, b, (dims, ((), ())), preferred_element_type=F32)


class Gather:
    def __init__(self, buf, sems, layer, slab, chips):
        self.buf, self.layer, self.chips = buf, layer, chips
        self.chip, self.core = slab // 2, slab % 2
        self.direct_send, self.direct_recv, self.pair_send, self.pair_recv = sems

    def slot(self, offset, core):
        return lax.rem(self.chip - offset + self.chips, self.chips) * 2 + core

    def direct(self, offset):
        mine = self.slot(0, self.core)
        there = lax.rem(self.chip + offset, self.chips) * 2 + self.core
        return pltpu.make_async_remote_copy(
            src_ref=self.buf.at[mine], dst_ref=self.buf.at[mine],
            send_sem=self.direct_send.at[offset], recv_sem=self.direct_recv.at[offset],
            device_id=(self.layer, there), device_id_type=MESH)

    def arrival(self, offset):
        here = self.slot(offset, self.core)
        return pltpu.make_async_remote_copy(
            src_ref=self.buf.at[here], dst_ref=self.buf.at[here],
            send_sem=self.direct_send.at[offset], recv_sem=self.direct_recv.at[offset],
            device_id=(self.layer, self.slot(0, 1 - self.core)), device_id_type=MESH)

    def pair(self, offset, core):
        here = self.slot(offset, core)
        return pltpu.make_async_remote_copy(
            src_ref=self.buf.at[here], dst_ref=self.buf.at[here],
            send_sem=self.pair_send.at[offset], recv_sem=self.pair_recv.at[offset],
            device_id=(self.layer, self.slot(0, 1 - self.core)), device_id_type=MESH)

    def order(self):
        out = []
        for k in range(1, self.chips // 2 + 1):
            out += sorted({k, self.chips - k})
        return out

    def start(self):
        for offset in self.order():
            self.direct(offset).start()
        self.pair(0, self.core).start()

    def take(self, offset):
        self.arrival(offset).wait_recv()
        self.pair(offset, self.core).start()

    def take_pair(self, offset):
        self.pair(offset, 1 - self.core).wait_recv()

    def finish(self):
        for offset in range(1, self.chips):
            self.direct(offset).wait_send()
        for offset in range(self.chips):
            self.pair(offset, self.core).wait_send()


def first_kernel(layers, slabs, act_ref, prior_ref, tgt_ref, ridge_ref,
                 x_out, xown_out, dir_out, d1_ref, r1_ref, w1_ref, rr_ref,
                 xs, xflat, r0, img, pbuf, acc, rrs, prior_sem, own_sem, lay_send, lay_recv, out_sem,
                 *sems):
    chips = slabs // 2
    width = tgt_ref.shape[1]
    layer, slab = lax.axis_index("layer"), lax.axis_index("slab")
    chip, core = slab // 2, slab % 2
    rows = act_ref.shape[1]
    tokens = layers * slabs * rows
    lam = ridge_ref[0]
    gx = Gather(xs, sems[0:4], layer, slab, chips)
    gr = Gather(r0, sems[4:8], layer, slab, chips)
    gi = Gather(img, sems[8:12], layer, slab, chips)

    order = [(0, 0), (0, 1)]
    for offset in gr.order():
        order += [(offset, 0), (offset, 1)]

    def slot_of(step):
        offset, other = order[step]
        return gr.slot(offset, 1 - core if other else core)

    def prior_copy(step):
        at = pl.multiple_of(slot_of(step) * width, width)
        return pltpu.make_async_copy(prior_ref.at[0, pl.ds(at, width), :], pbuf.at[step % 2], prior_sem.at[step % 2])

    prior_copy(0).start()
    own = pltpu.make_async_copy(act_ref.at[layer], xs.at[slab, layer], own_sem)
    own.start()
    r0[slab] = tgt_ref[0].T

    barrier = pltpu.get_barrier_semaphore()
    partners = [(lax.rem(layer + k, layers), slab) for k in range(1, layers)]
    partners += [(layer, lax.rem(chip + k, chips) * 2 + core) for k in range(1, chips)]
    partners += [(layer, chip * 2 + 1 - core)]
    for partner in partners:
        pl.semaphore_signal(barrier, inc=1, device_id=partner, device_id_type=MESH)
    pl.semaphore_wait(barrier, len(partners))

    def to_layer(k):
        there = lax.rem(layer + k, layers)
        return pltpu.make_async_remote_copy(
            src_ref=act_ref.at[there], dst_ref=xs.at[slab, layer],
            send_sem=lay_send.at[k], recv_sem=lay_recv.at[k],
            device_id=(there, slab), device_id_type=MESH)

    def from_layer(k):
        there = lax.rem(layer - k + layers, layers)
        return pltpu.make_async_remote_copy(
            src_ref=act_ref.at[there], dst_ref=xs.at[slab, there],
            send_sem=lay_send.at[k], recv_sem=lay_recv.at[k],
            device_id=(there, slab), device_id_type=MESH)

    for k in range(1, layers):
        to_layer(k).start()
    gr.start()
    own.wait()
    for k in range(1, layers):
        from_layer(k).wait_recv()
    gx.start()

    acc[...] = jnp.zeros_like(acc)
    rrs[...] = jnp.zeros_like(rrs)
    depth = min(256, width)
    half = acc.shape[0] // 2

    for step in range(len(order)):
        offset, other = order[step]
        if step + 1 < len(order):
            prior_copy(step + 1).start()
        if other:
            gr.take_pair(offset)
        elif offset:
            gr.take(offset)
        at_slot = slot_of(step)
        prior_copy(step).wait()

        @pl.loop(0, width // depth)
        def _(i):
            at = pl.multiple_of(i * depth, depth)
            v = r0[at_slot, :, pl.ds(at, depth)]
            vhi, vlo = split(v)
            ghi, glo = split(pbuf[step % 2, pl.ds(at, depth), :])
            acc[...] += dot(jnp.concatenate([vhi, vlo], axis=0), ghi)
            acc[:half, :] += dot(vhi, glo)
            rrs[0] += jnp.sum(v * v, axis=1, keepdims=True)

    def flatten(at_slot):
        at = pl.multiple_of(at_slot * (layers * rows), layers * rows)
        block = xs[at_slot].astype(F32)
        xflat[pl.ds(at, layers * rows), :] = block.reshape(layers * rows, block.shape[2]).astype(BF16)

    flatten(slab)
    gx.take_pair(0)
    flatten(gx.slot(0, 1 - core))
    for offset in gx.order():
        gx.take(offset)
        flatten(gx.slot(offset, core))
        gx.take_pair(offset)
        flatten(gx.slot(offset, 1 - core))
    own_at = pl.multiple_of(slab * width, width)
    x_copy = pltpu.make_async_copy(xflat, x_out, out_sem.at[0])
    xown_copy = pltpu.make_async_copy(xflat.at[:, pl.ds(own_at, width)], xown_out, out_sem.at[1])
    x_copy.start()
    xown_copy.start()

    def project(k, total):
        at = pl.multiple_of(k * width, width)
        both = jnp.concatenate(split(r0[k]), axis=0)
        return total + dot(both, xflat[:, pl.ds(at, width)], ((1,), (1,)))

    mix = lax.fori_loop(0, slabs, project, jnp.zeros((2 * half, tokens), F32))
    shi, slo = split(mix[:half] + mix[half:])
    xown = xflat[:, pl.ds(own_at, width)]
    total = acc[:half, :] + acc[half:, :] + dot(shi, xown) + dot(slo, xown)
    img[slab] = total / tokens + lam * r0[slab]

    gi.start()
    rrs[1] = jnp.sum(r0[slab] * img[slab], axis=1, keepdims=True)

    def curve(at_slot):
        rrs[1] += jnp.sum(r0[at_slot] * img[at_slot], axis=1, keepdims=True)

    gi.take_pair(0)
    curve(gi.slot(0, 1 - core))
    for offset in gi.order():
        gi.take(offset)
        curve(gi.slot(offset, core))
        gi.take_pair(offset)
        curve(gi.slot(offset, 1 - core))
    gx.finish()
    gr.finish()
    gi.finish()
    for k in range(1, layers):
        to_layer(k).wait_send()

    alpha = rrs[0] / rrs[1]
    rrs[2] = jnp.zeros_like(rrs[2])

    @pl.loop(0, slabs)
    def _(k):
        now = r0[k] - alpha * img[k]
        img[k] = now
        rrs[2] += jnp.sum(now * now, axis=1, keepdims=True)

    beta = rrs[2] / rrs[0]

    @pl.loop(0, slabs)
    def _(k):
        hi, lo = split(img[k] + beta * r0[k])
        at = pl.multiple_of(k * width, width)
        dir_out[:half, pl.ds(at, width)] = hi
        dir_out[half:, pl.ds(at, width)] = lo

    r1_ref[...] = img[slab]
    d1_ref[...] = img[slab] + beta * r0[slab]
    w1_ref[...] = alpha * r0[slab]
    rr_ref[...] = rrs[2]
    x_copy.wait()
    xown_copy.wait()


def gram_kernel(prior_ref, x_ref, xown_ref, dir_ref, gram_ref, image_ref, acc):
    @pl.when(pl.program_id(0) == 0)
    def _():
        acc[...] = jnp.zeros_like(acc)

    half = acc.shape[0] // 2
    depth = 256

    @pl.loop(0, prior_ref.shape[1] // depth)
    def _(i):
        at = pl.multiple_of(i * depth, depth)
        block = prior_ref[0, pl.ds(at, depth), :] + dot(x_ref[:, pl.ds(at, depth)], xown_ref[...], ((0,), (0,)))
        gram_ref[0, pl.ds(at, depth), :] = block
        ghi, glo = split(block)
        acc[...] += dot(dir_ref[:, pl.ds(at, depth)], ghi)
        acc[:half, :] += dot(dir_ref[:half, pl.ds(at, depth)], glo)

    @pl.when(pl.program_id(0) == pl.num_programs(0) - 1)
    def _():
        image_ref[...] = acc[:half, :] + acc[half:, :]


def last_kernel(slabs, tokens, raw_ref, d1_ref, r1_ref, w1_ref, rr_ref, ridge_ref,
                w_ref, r_ref, parts, send_sem, recv_sem):
    layer, slab = lax.axis_index("layer"), lax.axis_index("slab")
    barrier = pltpu.get_barrier_semaphore()
    for k in range(1, slabs):
        pl.semaphore_signal(barrier, inc=1, device_id=(layer, lax.rem(slab + k, slabs)), device_id_type=MESH)
    d1 = d1_ref[...]
    image = raw_ref[...] / tokens + ridge_ref[0] * d1
    curve = jnp.sum(d1 * image, axis=1, keepdims=True)
    wide = jnp.broadcast_to(curve, (curve.shape[0], 128))
    parts[0] = wide.T[:8]
    pl.semaphore_wait(barrier, slabs - 1)

    def send(k):
        return pltpu.make_async_remote_copy(
            src_ref=parts.at[0], dst_ref=parts.at[k], send_sem=send_sem.at[k], recv_sem=recv_sem.at[k],
            device_id=(layer, lax.rem(slab + k, slabs)), device_id_type=MESH)

    for k in range(1, slabs):
        send(k).start()
    for k in range(1, slabs):
        send(k).wait()
    total = jnp.sum(parts[...], axis=0)[:1]
    total = jnp.broadcast_to(total, (128, total.shape[1])).T[:, :1]
    alpha = rr_ref[...] / total
    w_ref[0] = (w1_ref[...] + alpha * d1).T
    r_ref[0] = (r1_ref[...] - alpha * image).T


def on_device(layers, slabs, activations, gram_prior, targets, ridge):
    size, width = gram_prior.shape[1], gram_prior.shape[2]
    count = targets.shape[2]
    rows = activations.shape[1]
    chips = slabs // 2
    tokens = layers * slabs * rows
    vmem, anywhere, smem = (pl.BlockSpec(memory_space=m) for m in (pltpu.VMEM, pl.ANY, pltpu.SMEM))
    block = jax.ShapeDtypeStruct((count, width), F32)
    dma = pltpu.SemaphoreType.DMA
    limit = 60 * 1024 * 1024
    gather_sems = [dma((chips,))] * 4
    x, xown, direction, d1, r1, w1, rr = pl.pallas_call(
        functools.partial(first_kernel, layers, slabs),
        out_shape=(
            jax.ShapeDtypeStruct((tokens, size), BF16),
            jax.ShapeDtypeStruct((tokens, width), BF16),
            jax.ShapeDtypeStruct((2 * count, size), BF16),
            block, block, block,
            jax.ShapeDtypeStruct((count, 1), F32),
        ),
        in_specs=[anywhere, anywhere, vmem, smem],
        out_specs=(anywhere, anywhere, vmem, vmem, vmem, vmem, vmem),
        scratch_shapes=[
            pltpu.VMEM((slabs, layers, rows, size), BF16),
            pltpu.VMEM((tokens, size), BF16),
            pltpu.VMEM((slabs, count, width), F32),
            pltpu.VMEM((slabs, count, width), F32),
            pltpu.VMEM((2, width, width), F32),
            pltpu.VMEM((2 * count, width), F32),
            pltpu.VMEM((3, count, 1), F32),
            dma((2,)), dma, dma((layers,)), dma((layers,)), dma((2,)),
        ] + gather_sems * 3,
        compiler_params=pltpu.CompilerParams(
            collective_id=0, has_side_effects=True, vmem_limit_bytes=limit),
        name="gather_and_first_step",
    )(activations, gram_prior, targets, ridge)

    step = min(512, size)
    gram, raw = pl.pallas_call(
        gram_kernel,
        grid=(size // step,),
        out_shape=(jax.ShapeDtypeStruct((1, size, width), F32), block),
        in_specs=[
            pl.BlockSpec((1, step, width), lambda i: (0, i, 0)),
            pl.BlockSpec((tokens, step), lambda i: (0, i)),
            pl.BlockSpec((tokens, width), lambda i: (0, 0)),
            pl.BlockSpec((2 * count, step), lambda i: (0, i)),
        ],
        out_specs=(
            pl.BlockSpec((1, step, width), lambda i: (0, i, 0)),
            pl.BlockSpec((count, width), lambda i: (0, 0)),
        ),
        scratch_shapes=[pltpu.VMEM((2 * count, width), F32)],
        compiler_params=pltpu.CompilerParams(vmem_limit_bytes=limit),
        name="gram_and_second_image",
    )(gram_prior, x, xown, direction)

    out = jax.ShapeDtypeStruct((1, width, count), F32)
    weights, resid = pl.pallas_call(
        functools.partial(last_kernel, slabs, tokens),
        out_shape=(out, out),
        in_specs=[vmem, vmem, vmem, vmem, vmem, smem],
        out_specs=(vmem, vmem),
        scratch_shapes=[pltpu.VMEM((slabs, 8, count), F32), dma((slabs,)), dma((slabs,))],
        compiler_params=pltpu.CompilerParams(collective_id=1, has_side_effects=True),
        name="second_step",
    )(raw, d1, r1, w1, rr, ridge)
    return gram, weights, resid


def solution(mesh):
    return jax.shard_map(
        functools.partial(on_device, mesh.shape["layer"], mesh.shape["slab"]),
        mesh=mesh,
        in_specs=(
            P(None, ("layer", "slab"), None),
            P("layer", None, "slab"),
            P("layer", "slab", None),
            P("layer"),
        ),
        out_specs=(P("layer", None, "slab"), P("layer", "slab", None), P("layer", "slab", None)),
        check_vma=False,
    )
```

```python
import functools
import jax
import jax.numpy as jnp
from jax import lax
from jax.experimental import pallas as pl
from jax.experimental.pallas import tpu as pltpu
from jax.sharding import PartitionSpec as P

MESH = pl.DeviceIdType.MESH
F32 = jnp.float32
BF16 = jnp.bfloat16


def split(x):
    hi = x.astype(BF16)
    return hi, (x - hi.astype(F32)).astype(BF16)


def dot(a, b, dims=((1,), (0,))):
    return lax.dot_general(a, b, (dims, ((), ())), preferred_element_type=F32)


class Gather:
    def __init__(self, buf, sems, layer, slab, chips):
        self.buf, self.layer, self.chips = buf, layer, chips
        self.chip, self.core = slab // 2, slab % 2
        self.direct_send, self.direct_recv, self.pair_send, self.pair_recv = sems

    def slot(self, offset, core):
        return lax.rem(self.chip - offset + self.chips, self.chips) * 2 + core

    def direct(self, offset):
        mine = self.slot(0, self.core)
        there = lax.rem(self.chip + offset, self.chips) * 2 + self.core
        return pltpu.make_async_remote_copy(
            src_ref=self.buf.at[mine], dst_ref=self.buf.at[mine],
            send_sem=self.direct_send.at[offset], recv_sem=self.direct_recv.at[offset],
            device_id=(self.layer, there), device_id_type=MESH)

    def arrival(self, offset):
        here = self.slot(offset, self.core)
        return pltpu.make_async_remote_copy(
            src_ref=self.buf.at[here], dst_ref=self.buf.at[here],
            send_sem=self.direct_send.at[offset], recv_sem=self.direct_recv.at[offset],
            device_id=(self.layer, self.slot(0, 1 - self.core)), device_id_type=MESH)

    def pair(self, offset, core):
        here = self.slot(offset, core)
        return pltpu.make_async_remote_copy(
            src_ref=self.buf.at[here], dst_ref=self.buf.at[here],
            send_sem=self.pair_send.at[offset], recv_sem=self.pair_recv.at[offset],
            device_id=(self.layer, self.slot(0, 1 - self.core)), device_id_type=MESH)

    def order(self):
        out = []
        for k in range(1, self.chips // 2 + 1):
            out += sorted({k, self.chips - k})
        return out

    def start(self):
        for offset in self.order():
            self.direct(offset).start()
        self.pair(0, self.core).start()

    def take(self, offset):
        self.arrival(offset).wait_recv()
        self.pair(offset, self.core).start()

    def take_pair(self, offset):
        self.pair(offset, 1 - self.core).wait_recv()

    def finish(self):
        for offset in range(1, self.chips):
            self.direct(offset).wait_send()
        for offset in range(self.chips):
            self.pair(offset, self.core).wait_send()


def first_kernel(layers, slabs, act_ref, prior_ref, tgt_ref, ridge_ref,
                 x_out, xown_out, r0_out, image_ref,
                 xs, xflat, r0, pbuf, acc, prior_sem, own_sem, lay_send, lay_recv, out_sem,
                 *sems):
    chips = slabs // 2
    width = tgt_ref.shape[1]
    layer, slab = lax.axis_index("layer"), lax.axis_index("slab")
    chip, core = slab // 2, slab % 2
    rows = act_ref.shape[1]
    tokens = layers * slabs * rows
    lam = ridge_ref[0]
    gx = Gather(xs, sems[0:4], layer, slab, chips)
    gr = Gather(r0, sems[4:8], layer, slab, chips)

    order = [(0, 0), (0, 1)]
    for offset in gr.order():
        order += [(offset, 0), (offset, 1)]

    def slot_of(step):
        offset, other = order[step]
        return gr.slot(offset, 1 - core if other else core)

    def prior_copy(step):
        at = pl.multiple_of(slot_of(step) * width, width)
        return pltpu.make_async_copy(prior_ref.at[0, pl.ds(at, width), :], pbuf.at[step % 2], prior_sem.at[step % 2])

    prior_copy(0).start()
    own = pltpu.make_async_copy(act_ref.at[layer], xs.at[slab, layer], own_sem)
    own.start()
    r0[slab] = tgt_ref[0].T

    barrier = pltpu.get_barrier_semaphore()
    partners = [(lax.rem(layer + k, layers), slab) for k in range(1, layers)]
    partners += [(layer, lax.rem(chip + k, chips) * 2 + core) for k in range(1, chips)]
    partners += [(layer, chip * 2 + 1 - core)]
    for partner in partners:
        pl.semaphore_signal(barrier, inc=1, device_id=partner, device_id_type=MESH)
    pl.semaphore_wait(barrier, len(partners))

    def to_layer(k):
        there = lax.rem(layer + k, layers)
        return pltpu.make_async_remote_copy(
            src_ref=act_ref.at[there], dst_ref=xs.at[slab, layer],
            send_sem=lay_send.at[k], recv_sem=lay_recv.at[k],
            device_id=(there, slab), device_id_type=MESH)

    def from_layer(k):
        there = lax.rem(layer - k + layers, layers)
        return pltpu.make_async_remote_copy(
            src_ref=act_ref.at[there], dst_ref=xs.at[slab, there],
            send_sem=lay_send.at[k], recv_sem=lay_recv.at[k],
            device_id=(there, slab), device_id_type=MESH)

    for k in range(1, layers):
        to_layer(k).start()
    gr.start()
    own.wait()
    for k in range(1, layers):
        from_layer(k).wait_recv()
    gx.start()

    acc[...] = jnp.zeros_like(acc)
    depth = min(256, width)
    half = acc.shape[0] // 2

    for step in range(len(order)):
        offset, other = order[step]
        if step + 1 < len(order):
            prior_copy(step + 1).start()
        if other:
            gr.take_pair(offset)
        elif offset:
            gr.take(offset)
        at_slot = slot_of(step)
        prior_copy(step).wait()

        @pl.loop(0, width // depth)
        def _(i):
            at = pl.multiple_of(i * depth, depth)
            v = r0[at_slot, :, pl.ds(at, depth)]
            vhi, vlo = split(v)
            ghi, glo = split(pbuf[step % 2, pl.ds(at, depth), :])
            acc[...] += dot(jnp.concatenate([vhi, vlo], axis=0), ghi)
            acc[:half, :] += dot(vhi, glo)

    r0_copy = pltpu.make_async_copy(r0, r0_out, out_sem.at[2])
    r0_copy.start()

    def flatten(at_slot):
        at = pl.multiple_of(at_slot * (layers * rows), layers * rows)
        block = xs[at_slot].astype(F32)
        xflat[pl.ds(at, layers * rows), :] = block.reshape(layers * rows, block.shape[2]).astype(BF16)

    flatten(slab)
    gx.take_pair(0)
    flatten(gx.slot(0, 1 - core))
    for offset in gx.order():
        gx.take(offset)
        flatten(gx.slot(offset, core))
        gx.take_pair(offset)
        flatten(gx.slot(offset, 1 - core))
    own_at = pl.multiple_of(slab * width, width)
    x_copy = pltpu.make_async_copy(xflat, x_out, out_sem.at[0])
    xown_copy = pltpu.make_async_copy(xflat.at[:, pl.ds(own_at, width)], xown_out, out_sem.at[1])
    x_copy.start()
    xown_copy.start()

    def project(k, total):
        at = pl.multiple_of(k * width, width)
        both = jnp.concatenate(split(r0[k]), axis=0)
        return total + dot(both, xflat[:, pl.ds(at, width)], ((1,), (1,)))

    mix = lax.fori_loop(0, slabs, project, jnp.zeros((2 * half, tokens), F32))
    shi, slo = split(mix[:half] + mix[half:])
    xown = xflat[:, pl.ds(own_at, width)]
    total = acc[:half, :] + acc[half:, :] + dot(shi, xown) + dot(slo, xown)
    image_ref[...] = total / tokens + lam * r0[slab]
    gx.finish()
    gr.finish()
    for k in range(1, layers):
        to_layer(k).wait_send()
    r0_copy.wait()
    x_copy.wait()
    xown_copy.wait()


def gram_kernel(prior_ref, x_ref, xown_ref, gram_ref):
    depth = 256
    for at in range(0, prior_ref.shape[1], depth):
        gram_ref[0, at:at + depth, :] = prior_ref[0, at:at + depth, :] + dot(
            x_ref[:, at:at + depth], xown_ref[...], ((0,), (0,)))


def second_kernel(slabs, tokens, gram_ref, r0_ref, img_ref, ridge_ref,
                  w_ref, r_ref, gbuf, acc, sums, parts, gram_sem, send_sem, recv_sem):
    layer, slab = lax.axis_index("layer"), lax.axis_index("slab")
    half, width = r0_ref.shape[1:]

    def gram_copy(k):
        return pltpu.make_async_copy(
            gram_ref.at[0, pl.ds(k * width, width), :], gbuf.at[k % 3], gram_sem.at[k % 3])

    for k in range(min(2, slabs)):
        gram_copy(k).start()
    barrier = pltpu.get_barrier_semaphore()
    for k in range(1, slabs):
        pl.semaphore_signal(barrier, inc=1, device_id=(layer, lax.rem(slab + k, slabs)), device_id_type=MESH)

    acc[...] = jnp.zeros_like(acc)
    sums[...] = jnp.zeros_like(sums)

    def lanes(x):
        return functools.reduce(jnp.add, [x[:, at:at + 128] for at in range(0, width, 128)])

    @pl.loop(0, slabs)
    def _(k):
        r0 = r0_ref[k]
        sums[0] += lanes(r0 * r0)
        sums[1] += lanes(r0 * img_ref[k])

    norm0 = jnp.sum(sums[0], axis=1, keepdims=True)
    alpha0 = norm0 / jnp.sum(sums[1], axis=1, keepdims=True)

    @pl.loop(0, slabs)
    def _(k):
        r1 = r0_ref[k] - alpha0 * img_ref[k]
        sums[2] += lanes(r1 * r1)

    norm1 = jnp.sum(sums[2], axis=1, keepdims=True)
    beta = norm1 / norm0
    depth = min(256, width)

    for k in range(slabs):
        if k + 2 < slabs:
            gram_copy(k + 2).start()
        gram_copy(k).wait()
        for at in range(0, width, depth):
            r0 = r0_ref[k, :, at:at + depth]
            vhi, vlo = split(r0 - alpha0 * img_ref[k, :, at:at + depth] + beta * r0)
            ghi, glo = split(gbuf[k % 3, at:at + depth, :])
            acc[...] += dot(jnp.concatenate([vhi, vlo], axis=0), ghi)
            acc[:half, :] += dot(vhi, glo)

    r0 = r0_ref[slab]
    r1 = r0 - alpha0 * img_ref[slab]
    d1 = r1 + beta * r0
    image = (acc[:half, :] + acc[half:, :]) / tokens + ridge_ref[0] * d1
    curve = jnp.sum(d1 * image, axis=1, keepdims=True)
    parts[0] = jnp.broadcast_to(curve, (half, 128)).T[:8]
    pl.semaphore_wait(barrier, slabs - 1)

    def send(k):
        return pltpu.make_async_remote_copy(
            src_ref=parts.at[0], dst_ref=parts.at[k], send_sem=send_sem.at[k], recv_sem=recv_sem.at[k],
            device_id=(layer, lax.rem(slab + k, slabs)), device_id_type=MESH)

    for k in range(1, slabs):
        send(k).start()
    for k in range(1, slabs):
        send(k).wait()
    total = jnp.sum(parts[...], axis=0)[:1]
    total = jnp.broadcast_to(total, (128, half)).T[:, :1]
    alpha1 = norm1 / total
    w_ref[0] = (alpha0 * r0 + alpha1 * d1).T
    r_ref[0] = (r1 - alpha1 * image).T


def on_device(layers, slabs, activations, gram_prior, targets, ridge):
    size, width = gram_prior.shape[1], gram_prior.shape[2]
    count = targets.shape[2]
    rows = activations.shape[1]
    chips = slabs // 2
    tokens = layers * slabs * rows
    vmem, anywhere, smem = (pl.BlockSpec(memory_space=m) for m in (pltpu.VMEM, pl.ANY, pltpu.SMEM))
    block = jax.ShapeDtypeStruct((count, width), F32)
    dma = pltpu.SemaphoreType.DMA
    limit = 60 * 1024 * 1024
    x, xown, r0, image = pl.pallas_call(
        functools.partial(first_kernel, layers, slabs),
        out_shape=(
            jax.ShapeDtypeStruct((tokens, size), BF16),
            jax.ShapeDtypeStruct((tokens, width), BF16),
            jax.ShapeDtypeStruct((slabs, count, width), F32),
            block,
        ),
        in_specs=[anywhere, anywhere, vmem, smem],
        out_specs=(anywhere, anywhere, anywhere, vmem),
        scratch_shapes=[
            pltpu.VMEM((slabs, layers, rows, size), BF16),
            pltpu.VMEM((tokens, size), BF16),
            pltpu.VMEM((slabs, count, width), F32),
            pltpu.VMEM((2, width, width), F32),
            pltpu.VMEM((2 * count, width), F32),
            dma((2,)), dma, dma((layers,)), dma((layers,)), dma((3,)),
        ] + [dma((chips,))] * 8,
        compiler_params=pltpu.CompilerParams(
            collective_id=0, has_side_effects=True, vmem_limit_bytes=limit),
        name="gather_and_first_image",
    )(activations, gram_prior, targets, ridge)
    images = lax.all_gather(image, "slab")

    step = min(512, size)
    gram = pl.pallas_call(
        gram_kernel,
        grid=(size // step,),
        out_shape=jax.ShapeDtypeStruct((1, size, width), F32),
        in_specs=[
            pl.BlockSpec((1, step, width), lambda i: (0, i, 0)),
            pl.BlockSpec((tokens, step), lambda i: (0, i)),
            pl.BlockSpec((tokens, width), lambda i: (0, 0)),
        ],
        out_specs=pl.BlockSpec((1, step, width), lambda i: (0, i, 0)),
        cost_estimate=pl.CostEstimate(
            flops=2 * size * width * tokens, bytes_accessed=8 * size * width, transcendentals=0),
        compiler_params=pltpu.CompilerParams(vmem_limit_bytes=limit),
        name="gram_update",
    )(gram_prior, x, xown)

    out = jax.ShapeDtypeStruct((1, width, count), F32)
    weights, resid = pl.pallas_call(
        functools.partial(second_kernel, slabs, tokens),
        out_shape=(out, out),
        in_specs=[anywhere, vmem, vmem, smem],
        out_specs=(vmem, vmem),
        scratch_shapes=[
            pltpu.VMEM((3, width, width), F32),
            pltpu.VMEM((2 * count, width), F32),
            pltpu.VMEM((3, count, 128), F32),
            pltpu.VMEM((slabs, 8, count), F32),
            dma((3,)), dma((slabs,)), dma((slabs,)),
        ],
        compiler_params=pltpu.CompilerParams(
            collective_id=1, has_side_effects=True, vmem_limit_bytes=limit),
        name="second_image_and_step",
    )(gram, r0, images, ridge)
    return gram, weights, resid


def solution(mesh):
    return jax.shard_map(
        functools.partial(on_device, mesh.shape["layer"], mesh.shape["slab"]),
        mesh=mesh,
        in_specs=(
            P(None, ("layer", "slab"), None),
            P("layer", None, "slab"),
            P("layer", "slab", None),
            P("layer"),
        ),
        out_specs=(P("layer", None, "slab"), P("layer", "slab", None), P("layer", "slab", None)),
        check_vma=False,
    )
```

```python
import functools
import jax
import jax.numpy as jnp
from jax import lax
from jax.experimental import pallas as pl
from jax.experimental.pallas import tpu as pltpu
from jax.sharding import PartitionSpec as P

MESH = pl.DeviceIdType.MESH
F32 = jnp.float32
BF16 = jnp.bfloat16


def split(x):
    hi = x.astype(BF16)
    return hi, (x - hi.astype(F32)).astype(BF16)


def dot(a, b, dims=((1,), (0,))):
    return lax.dot_general(a, b, (dims, ((), ())), preferred_element_type=F32)


class Gather:
    def __init__(self, buf, sems, layer, slab, chips):
        self.buf, self.layer, self.chips = buf, layer, chips
        self.chip, self.core = slab // 2, slab % 2
        self.direct_send, self.direct_recv, self.pair_send, self.pair_recv = sems

    def slot(self, offset, core):
        return lax.rem(self.chip - offset + self.chips, self.chips) * 2 + core

    def direct(self, offset):
        mine = self.slot(0, self.core)
        there = lax.rem(self.chip + offset, self.chips) * 2 + self.core
        return pltpu.make_async_remote_copy(
            src_ref=self.buf.at[mine], dst_ref=self.buf.at[mine],
            send_sem=self.direct_send.at[offset], recv_sem=self.direct_recv.at[offset],
            device_id=(self.layer, there), device_id_type=MESH)

    def arrival(self, offset):
        here = self.slot(offset, self.core)
        return pltpu.make_async_remote_copy(
            src_ref=self.buf.at[here], dst_ref=self.buf.at[here],
            send_sem=self.direct_send.at[offset], recv_sem=self.direct_recv.at[offset],
            device_id=(self.layer, self.slot(0, 1 - self.core)), device_id_type=MESH)

    def pair(self, offset, core):
        here = self.slot(offset, core)
        return pltpu.make_async_remote_copy(
            src_ref=self.buf.at[here], dst_ref=self.buf.at[here],
            send_sem=self.pair_send.at[offset], recv_sem=self.pair_recv.at[offset],
            device_id=(self.layer, self.slot(0, 1 - self.core)), device_id_type=MESH)

    def order(self):
        out = []
        for k in range(1, self.chips // 2 + 1):
            out += sorted({k, self.chips - k})
        return out

    def start(self):
        for offset in self.order():
            self.direct(offset).start()
        self.pair(0, self.core).start()

    def take(self, offset):
        self.arrival(offset).wait_recv()
        self.pair(offset, self.core).start()

    def take_pair(self, offset):
        self.pair(offset, 1 - self.core).wait_recv()

    def finish(self):
        for offset in range(1, self.chips):
            self.direct(offset).wait_send()
        for offset in range(self.chips):
            self.pair(offset, self.core).wait_send()


def first_kernel(layers, slabs, act_ref, prior_ref, tgt_ref, ridge_ref,
                 x_out, xown_out, r0_out, image_ref,
                 xs, xflat, r0, pbuf, acc, prior_sem, own_sem, lay_send, lay_recv, out_sem,
                 *sems):
    chips = slabs // 2
    width = tgt_ref.shape[1]
    layer, slab = lax.axis_index("layer"), lax.axis_index("slab")
    chip, core = slab // 2, slab % 2
    rows = act_ref.shape[1]
    tokens = layers * slabs * rows
    lam = ridge_ref[0]
    gx = Gather(xs, sems[0:4], layer, slab, chips)
    gr = Gather(r0, sems[4:8], layer, slab, chips)

    order = [(0, 0), (0, 1)]
    for offset in gr.order():
        order += [(offset, 0), (offset, 1)]

    def slot_of(step):
        offset, other = order[step]
        return gr.slot(offset, 1 - core if other else core)

    def prior_copy(step):
        at = pl.multiple_of(slot_of(step) * width, width)
        return pltpu.make_async_copy(prior_ref.at[0, pl.ds(at, width), :], pbuf.at[step % 2], prior_sem.at[step % 2])

    prior_copy(0).start()
    own = pltpu.make_async_copy(act_ref.at[layer], xs.at[slab, layer], own_sem)
    own.start()
    r0[slab] = tgt_ref[0].T

    barrier = pltpu.get_barrier_semaphore()
    partners = [(lax.rem(layer + k, layers), slab) for k in range(1, layers)]
    partners += [(layer, lax.rem(chip + k, chips) * 2 + core) for k in range(1, chips)]
    partners += [(layer, chip * 2 + 1 - core)]
    for partner in partners:
        pl.semaphore_signal(barrier, inc=1, device_id=partner, device_id_type=MESH)
    pl.semaphore_wait(barrier, len(partners))

    def to_layer(k):
        there = lax.rem(layer + k, layers)
        return pltpu.make_async_remote_copy(
            src_ref=act_ref.at[there], dst_ref=xs.at[slab, layer],
            send_sem=lay_send.at[k], recv_sem=lay_recv.at[k],
            device_id=(there, slab), device_id_type=MESH)

    def from_layer(k):
        there = lax.rem(layer - k + layers, layers)
        return pltpu.make_async_remote_copy(
            src_ref=act_ref.at[there], dst_ref=xs.at[slab, there],
            send_sem=lay_send.at[k], recv_sem=lay_recv.at[k],
            device_id=(there, slab), device_id_type=MESH)

    for k in range(1, layers):
        to_layer(k).start()
    gr.start()
    own.wait()
    for k in range(1, layers):
        from_layer(k).wait_recv()
    gx.start()

    acc[...] = jnp.zeros_like(acc)
    depth = min(256, width)
    half = acc.shape[0] // 2

    for step in range(len(order)):
        offset, other = order[step]
        if step + 1 < len(order):
            prior_copy(step + 1).start()
        if other:
            gr.take_pair(offset)
        elif offset:
            gr.take(offset)
        at_slot = slot_of(step)
        prior_copy(step).wait()

        @pl.loop(0, width // depth)
        def _(i):
            at = pl.multiple_of(i * depth, depth)
            v = r0[at_slot, :, pl.ds(at, depth)]
            vhi, vlo = split(v)
            ghi, glo = split(pbuf[step % 2, pl.ds(at, depth), :])
            acc[...] += dot(jnp.concatenate([vhi, vlo], axis=0), ghi)
            acc[:half, :] += dot(vhi, glo)

    r0_copy = pltpu.make_async_copy(r0, r0_out, out_sem.at[2])
    r0_copy.start()

    def flatten(at_slot):
        at = pl.multiple_of(at_slot * (layers * rows), layers * rows)
        block = xs[at_slot].astype(F32)
        xflat[pl.ds(at, layers * rows), :] = block.reshape(layers * rows, block.shape[2]).astype(BF16)

    flatten(slab)
    gx.take_pair(0)
    flatten(gx.slot(0, 1 - core))
    for offset in gx.order():
        gx.take(offset)
        flatten(gx.slot(offset, core))
        gx.take_pair(offset)
        flatten(gx.slot(offset, 1 - core))
    own_at = pl.multiple_of(slab * width, width)
    x_copy = pltpu.make_async_copy(xflat, x_out, out_sem.at[0])
    xown_copy = pltpu.make_async_copy(xflat.at[:, pl.ds(own_at, width)], xown_out, out_sem.at[1])
    x_copy.start()
    xown_copy.start()

    def project(k, total):
        at = pl.multiple_of(k * width, width)
        both = jnp.concatenate(split(r0[k]), axis=0)
        return total + dot(both, xflat[:, pl.ds(at, width)], ((1,), (1,)))

    mix = lax.fori_loop(0, slabs, project, jnp.zeros((2 * half, tokens), F32))
    shi, slo = split(mix[:half] + mix[half:])
    xown = xflat[:, pl.ds(own_at, width)]
    total = acc[:half, :] + acc[half:, :] + dot(shi, xown) + dot(slo, xown)
    image_ref[...] = total / tokens + lam * r0[slab]
    gx.finish()
    gr.finish()
    for k in range(1, layers):
        to_layer(k).wait_send()
    r0_copy.wait()
    x_copy.wait()
    xown_copy.wait()


def gram_kernel(prior_ref, x_ref, xown_ref, gram_ref):
    depth = 256
    for at in range(0, prior_ref.shape[1], depth):
        gram_ref[0, at:at + depth, :] = prior_ref[0, at:at + depth, :] + dot(
            x_ref[:, at:at + depth], xown_ref[...], ((0,), (0,)))


def second_kernel(slabs, tokens, gram_ref, r0_ref, img_ref, ridge_ref,
                  w_ref, r_ref, gbuf, acc, sums, parts, gram_sem, send_sem, recv_sem):
    layer, slab = lax.axis_index("layer"), lax.axis_index("slab")
    half, width = r0_ref.shape[1:]

    def gram_copy(k):
        return pltpu.make_async_copy(
            gram_ref.at[0, pl.ds(k * width, width), :], gbuf.at[k % 3], gram_sem.at[k % 3])

    for k in range(min(2, slabs)):
        gram_copy(k).start()
    barrier = pltpu.get_barrier_semaphore()
    for k in range(1, slabs):
        pl.semaphore_signal(barrier, inc=1, device_id=(layer, lax.rem(slab + k, slabs)), device_id_type=MESH)

    acc[...] = jnp.zeros_like(acc)
    sums[...] = jnp.zeros_like(sums)

    def lanes(x):
        return functools.reduce(jnp.add, [x[:, at:at + 128] for at in range(0, width, 128)])

    @pl.loop(0, slabs)
    def _(k):
        r0 = r0_ref[k]
        sums[0] += lanes(r0 * r0)
        sums[1] += lanes(r0 * img_ref[k])

    norm0 = jnp.sum(sums[0], axis=1, keepdims=True)
    alpha0 = norm0 / jnp.sum(sums[1], axis=1, keepdims=True)

    @pl.loop(0, slabs)
    def _(k):
        r1 = r0_ref[k] - alpha0 * img_ref[k]
        sums[2] += lanes(r1 * r1)

    norm1 = jnp.sum(sums[2], axis=1, keepdims=True)
    beta = norm1 / norm0
    depth = min(256, width)

    for k in range(slabs):
        if k + 2 < slabs:
            gram_copy(k + 2).start()
        gram_copy(k).wait()
        for at in range(0, width, depth):
            r0 = r0_ref[k, :, at:at + depth]
            vhi, vlo = split(r0 - alpha0 * img_ref[k, :, at:at + depth] + beta * r0)
            ghi, glo = split(gbuf[k % 3, at:at + depth, :])
            acc[...] += dot(jnp.concatenate([vhi, vlo], axis=0), ghi)
            acc[:half, :] += dot(vhi, glo)

    r0 = r0_ref[slab]
    r1 = r0 - alpha0 * img_ref[slab]
    d1 = r1 + beta * r0
    image = (acc[:half, :] + acc[half:, :]) / tokens + ridge_ref[0] * d1
    curve = jnp.sum(d1 * image, axis=1, keepdims=True)
    parts[0] = jnp.broadcast_to(curve, (half, 128)).T[:8]
    pl.semaphore_wait(barrier, slabs - 1)

    def send(k):
        return pltpu.make_async_remote_copy(
            src_ref=parts.at[0], dst_ref=parts.at[k], send_sem=send_sem.at[k], recv_sem=recv_sem.at[k],
            device_id=(layer, lax.rem(slab + k, slabs)), device_id_type=MESH)

    for k in range(1, slabs):
        send(k).start()
    for k in range(1, slabs):
        send(k).wait()
    total = jnp.sum(parts[...], axis=0)[:1]
    total = jnp.broadcast_to(total, (128, half)).T[:, :1]
    alpha1 = norm1 / total
    w_ref[...] = alpha0 * r0 + alpha1 * d1
    r_ref[...] = r1 - alpha1 * image


def on_device(layers, slabs, activations, gram_prior, targets, ridge):
    size, width = gram_prior.shape[1], gram_prior.shape[2]
    count = targets.shape[2]
    rows = activations.shape[1]
    chips = slabs // 2
    tokens = layers * slabs * rows
    vmem, anywhere, smem = (pl.BlockSpec(memory_space=m) for m in (pltpu.VMEM, pl.ANY, pltpu.SMEM))
    block = jax.ShapeDtypeStruct((count, width), F32)
    dma = pltpu.SemaphoreType.DMA
    limit = 60 * 1024 * 1024
    x, xown, r0, image = pl.pallas_call(
        functools.partial(first_kernel, layers, slabs),
        out_shape=(
            jax.ShapeDtypeStruct((tokens, size), BF16),
            jax.ShapeDtypeStruct((tokens, width), BF16),
            jax.ShapeDtypeStruct((slabs, count, width), F32),
            block,
        ),
        in_specs=[anywhere, anywhere, vmem, smem],
        out_specs=(anywhere, anywhere, anywhere, vmem),
        scratch_shapes=[
            pltpu.VMEM((slabs, layers, rows, size), BF16),
            pltpu.VMEM((tokens, size), BF16),
            pltpu.VMEM((slabs, count, width), F32),
            pltpu.VMEM((2, width, width), F32),
            pltpu.VMEM((2 * count, width), F32),
            dma((2,)), dma, dma((layers,)), dma((layers,)), dma((3,)),
        ] + [dma((chips,))] * 8,
        compiler_params=pltpu.CompilerParams(
            collective_id=0, has_side_effects=True, vmem_limit_bytes=limit),
        name="gather_and_first_image",
    )(activations, gram_prior, targets, ridge)
    images = lax.all_gather(image, "slab")

    step = min(512, size)
    gram = pl.pallas_call(
        gram_kernel,
        grid=(size // step,),
        out_shape=jax.ShapeDtypeStruct((1, size, width), F32),
        in_specs=[
            pl.BlockSpec((1, step, width), lambda i: (0, i, 0)),
            pl.BlockSpec((tokens, step), lambda i: (0, i)),
            pl.BlockSpec((tokens, width), lambda i: (0, 0)),
        ],
        out_specs=pl.BlockSpec((1, step, width), lambda i: (0, i, 0)),
        cost_estimate=pl.CostEstimate(
            flops=2 * size * width * tokens, bytes_accessed=8 * size * width, transcendentals=0),
        compiler_params=pltpu.CompilerParams(vmem_limit_bytes=limit),
        name="gram_update",
    )(gram_prior, x, xown)

    weights, resid = pl.pallas_call(
        functools.partial(second_kernel, slabs, tokens),
        out_shape=(block, block),
        in_specs=[anywhere, vmem, vmem, smem],
        out_specs=(vmem, vmem),
        scratch_shapes=[
            pltpu.VMEM((3, width, width), F32),
            pltpu.VMEM((2 * count, width), F32),
            pltpu.VMEM((3, count, 128), F32),
            pltpu.VMEM((slabs, 8, count), F32),
            dma((3,)), dma((slabs,)), dma((slabs,)),
        ],
        compiler_params=pltpu.CompilerParams(
            collective_id=1, has_side_effects=True, vmem_limit_bytes=limit),
        name="second_image_and_step",
    )(gram, r0, images, ridge)
    return gram, weights.T[None], resid.T[None]


def solution(mesh):
    return jax.shard_map(
        functools.partial(on_device, mesh.shape["layer"], mesh.shape["slab"]),
        mesh=mesh,
        in_specs=(
            P(None, ("layer", "slab"), None),
            P("layer", None, "slab"),
            P("layer", "slab", None),
            P("layer"),
        ),
        out_specs=(P("layer", None, "slab"), P("layer", "slab", None), P("layer", "slab", None)),
        check_vma=False,
    )
```
